32 devices in a mesh: section: 16 (over z, x, core), expert: 2 (over y).
Axes of the slice: x: 2, y: 2, z: 4, core: 2. Of those that a mesh axis runs over, the one named last changes fastest.
Arguments:
- tokens: bfloat16 [128, 3072], P('expert', 'section'), may hold values from -6 to 6
- routes: int32 [128, 2], P('expert'), may hold values from 0 to 7, all different within a row; in each aligned block of 64 rows (0 to 63, 64 to 127, ...) at most 20 rows name the same one
- combine: float32 [128, 2], P('expert'), may hold values from 0.1 to 1
- w_gate: bfloat16 [8, 3072, 8192], P('expert', None, 'section'), may hold values from -0.109375 to 0.109375
- w_up: bfloat16 [8, 3072, 8192], P('expert', None, 'section'), may hold values from -0.109375 to 0.109375
- w_down: bfloat16 [8, 8192, 3072], P('expert', 'section'), may hold values from -0.0625 to 0.0625
- cotangent: bfloat16 [128, 3072], P('expert', 'section'), may hold values from -6 to 6
Outputs:
- mixed: bfloat16 [128, 3072], P('expert', 'section')
- d_tokens: bfloat16 [128, 3072], P('expert', 'section')
- d_combine: float32 [128, 2], P('expert')
- grad_gate: bfloat16 [8, 3072, 8192], P('expert', None, 'section')
- grad_up: bfloat16 [8, 3072, 8192], P('expert', None, 'section')
- grad_down: bfloat16 [8, 8192, 3072], P('expert', 'section')
The draws below stay inside these ranges and needn't reach their ends.
Inputs may be any that keep to these rules, and one draw needn't show every extreme that they name: `routes`: each row names 2 different experts. In the 64 rows held by one index of the `expert` axis, no expert is named more than 20 times.
All inputs are finite; a program needn't handle non-finite values.
Results may differ from the reference program's by a relative error of at most 0.0065.
Values may be sent and summed in bfloat16 or wider, within the bound.
A program may use at most 192 MiB of HBM per device.

```python
import math
import jax
import jax.numpy as jnp
import numpy as np
from jax import lax

D = 3072
FF = 8192
EXPERTS = 8
TOPK = 2
TOK_E = 64
CAP = 20
TOKENS = 128
N_EXPERT = 2


def shard_levels(rng, extent, split, least, top_value):
    factor_of = 1.0
    for dim, parts in split:
        steps = jax.random.uniform(jax.random.fold_in(jax.random.fold_in(rng, 6), dim), (parts,), jnp.float32, least / len(split), top_value / len(split))
        factor_of = factor_of * jnp.repeat(jnp.exp(steps), extent[dim] // parts).reshape((-1,) + (1,) * (len(extent) - 1 - dim))
    return factor_of


def assign_block(key, own, number, rows, number_of, top, limit, slope):
    ranking = jax.random.permutation(key, number_of)
    crowded, common = shares(number_of, rows * top, limit, slope, True), shares(number_of, rows * top, limit, slope, False)
    places = jnp.arange(number_of)

    def named(tallies, offset_by):
        used = int((tallies > 0).sum())
        fixed = max(1, used // 4)
        passed = fixed + (places - fixed + offset_by * (used - fixed)) % max(1, number_of - fixed)
        return jnp.zeros((number_of,), jnp.int32).at[ranking[jnp.where(places < fixed, places, passed)]].set(jnp.asarray(tallies, jnp.int32))

    tallies = jnp.where(number % 4 == 0, named(crowded, number // 4), named(common, number - number // 4 - 1))
    mixed = jax.random.permutation(jax.random.fold_in(own, 3), number_of)
    source_of, receiver = mixed[0:number_of // 2 * 2:2], mixed[1:number_of // 2 * 2:2]
    room = jnp.minimum(tallies[source_of] - 1, limit - tallies[receiver]) // 2
    room = jnp.where((source_of == ranking[0]) | (receiver == ranking[0]) | (tallies[receiver] == 0), 0, jnp.maximum(room, 0))
    passed = jax.random.randint(jax.random.fold_in(own, 4), (number_of // 2,), 0, 1 << 20) % (room + 1)
    tallies = tallies.at[source_of].add(-passed).at[receiver].add(passed)
    members = jnp.searchsorted(jnp.cumsum(tallies), jnp.arange(rows * top), side="right").astype(jnp.int32)
    grid = members.reshape(top, rows).T
    grid = grid[jax.random.permutation(jax.random.fold_in(own, 1), rows)]
    offset_by = jax.random.randint(jax.random.fold_in(own, 2), (rows, 1), 0, top)
    return jnp.take_along_axis(grid, (jnp.arange(top)[None, :] + offset_by) % top, axis=1)


def shares(count, total, most, skew, full):
    weights = [(1 << 20) // math.isqrt(standing ** skew) + 1 for standing in range(1, count + 1)]
    largest = most if full else min(most, max(-(-total // count), total * weights[0] // sum(weights)))
    least = 1 if total - largest >= count - 1 else 0
    holding, spare = [largest] + [least] * (count - 1), total - largest - least * (count - 1)
    while spare > 0:
        free = [i for i in range(1, count) if holding[i] < largest] or [i for i in range(1, count) if holding[i] < most]
        mass, budget = sum([weights[i] for i in free]), spare
        for i in free:
            extra = min(most - holding[i], max(1, budget * weights[i] // mass), spare)
            holding[i] = holding[i] + extra
            spare = spare - extra
    return np.array(holding)


def gaussian(key, dims, deviation, bound, cuts=(), kind=jnp.bfloat16):
    result = deviation * jax.random.normal(key, dims, jnp.float32)
    if cuts:
        result = result * shard_levels(key, dims, cuts, -0.22, 0.18)
    return jnp.clip(result, -bound, bound).astype(kind)


def setup_inputs(seed: int = 0) -> dict:
    arg_keys = jax.random.split(jax.random.key(seed), 8)
    tokens = gaussian(arg_keys[0], (TOKENS, D), 1.0, 6.0, ((0, 2), (1, 16)))
    routes_keys = jax.random.split(jax.random.fold_in(arg_keys[1], 1), TOKENS // TOK_E)
    routes_turns = jax.random.permutation(jax.random.fold_in(arg_keys[1], 3), TOKENS // TOK_E)
    routes = jax.vmap(lambda own, number: assign_block(jax.random.fold_in(arg_keys[1], 2), own, number, TOK_E, EXPERTS, TOPK, CAP, 2))(routes_keys, routes_turns).reshape((TOKENS, TOPK))
    combine = jnp.clip(jnp.exp(math.log(1.0) - 2.3025851 * jax.random.uniform(arg_keys[2], (TOKENS, TOPK), jnp.float32) ** shard_levels(arg_keys[2], (TOKENS, TOPK), ((0, 2),), -0.2, 0.2)), 0.1, 1.0)
    w_gate = gaussian(arg_keys[3], (EXPERTS, D, FF), D ** -0.5, 0.109375, ((0, 2), (2, 16)))
    w_up = gaussian(arg_keys[4], (EXPERTS, D, FF), D ** -0.5, 0.109375, ((0, 2), (2, 16)))
    w_down = gaussian(arg_keys[5], (EXPERTS, FF, D), FF ** -0.5, 0.0625, ((0, 2), (1, 16)))
    cotangent = gaussian(arg_keys[6], (TOKENS, D), 1.0, 6.0, ((0, 2), (1, 16)))
    return dict(tokens=tokens, routes=routes, combine=combine, w_gate=w_gate, w_up=w_up, w_down=w_down, cotangent=cotangent)


def slot_tables(routes):
    ids = routes.reshape(N_EXPERT, TOK_E * TOPK).astype(jnp.int32)
    onehot = (ids[:, :, None] == jnp.arange(EXPERTS, dtype=jnp.int32)[None, None, :]).astype(jnp.int32)
    earlier = jnp.cumsum(onehot, axis=1) - onehot
    slot = jnp.sum(earlier * onehot, axis=2).astype(jnp.int32)
    group = jnp.broadcast_to(jnp.arange(N_EXPERT, dtype=jnp.int32)[:, None], ids.shape)
    return ids, group, slot


def reference(tokens, routes, combine, w_gate, w_up, w_down, cotangent):
    ids, group, slot = slot_tables(routes)
    repeated = jnp.repeat(tokens.reshape(N_EXPERT, TOK_E, D), TOPK, axis=1)
    expert_in = jnp.zeros((EXPERTS, N_EXPERT, CAP, D), jnp.bfloat16).at[ids, group, slot].set(repeated)
    expert_in = expert_in.reshape(EXPERTS, N_EXPERT * CAP, D)

    def forward(packed):
        inputs, wg, wu, wd = packed
        gate = jnp.dot(inputs, wg, preferred_element_type=jnp.float32)
        up = jnp.dot(inputs, wu, preferred_element_type=jnp.float32)
        hidden = (jax.nn.silu(gate) * up).astype(jnp.bfloat16)
        out = jnp.dot(hidden, wd, preferred_element_type=jnp.float32).astype(jnp.bfloat16)
        return out, gate, up

    expert_out, gate, up = lax.map(forward, (expert_in, w_gate, w_up, w_down))
    rows = expert_out.reshape(EXPERTS, N_EXPERT, CAP, D)[ids, group, slot].astype(jnp.float32)
    rows = rows.reshape(TOKENS, TOPK, D)
    mixed = jnp.sum(combine[:, :, None] * rows, axis=1).astype(jnp.bfloat16)
    cot = cotangent.astype(jnp.float32)
    d_combine = jnp.sum(rows * cot[:, None, :], axis=2)
    scaled = (combine[:, :, None] * cot[:, None, :]).reshape(N_EXPERT, TOK_E * TOPK, D)
    d_out = jnp.zeros((EXPERTS, N_EXPERT, CAP, D), jnp.float32).at[ids, group, slot].set(scaled)
    d_out = d_out.astype(jnp.bfloat16).reshape(EXPERTS, N_EXPERT * CAP, D)

    def backward(packed):
        inputs, wg, wu, wd, gate_e, up_e, dout = packed
        sig = jax.nn.sigmoid(gate_e)
        act = gate_e * sig
        hidden = (act * up_e).astype(jnp.bfloat16)
        d_hidden = jnp.dot(dout, wd.T, preferred_element_type=jnp.float32)
        d_gate = (d_hidden * up_e * sig * (1.0 + gate_e * (1.0 - sig))).astype(jnp.bfloat16)
        d_up = (d_hidden * act).astype(jnp.bfloat16)
        g_down = jnp.dot(hidden.T, dout, preferred_element_type=jnp.float32).astype(jnp.bfloat16)
        g_gate = jnp.dot(inputs.T, d_gate, preferred_element_type=jnp.float32).astype(jnp.bfloat16)
        g_up = jnp.dot(inputs.T, d_up, preferred_element_type=jnp.float32).astype(jnp.bfloat16)
        d_in = (jnp.dot(d_gate, wg.T, preferred_element_type=jnp.float32)
                + jnp.dot(d_up, wu.T, preferred_element_type=jnp.float32)).astype(jnp.bfloat16)
        return g_gate, g_up, g_down, d_in

    grad_gate, grad_up, grad_down, d_in = lax.map(backward, (expert_in, w_gate, w_up, w_down, gate, up, d_out))
    back_rows = d_in.reshape(EXPERTS, N_EXPERT, CAP, D)[ids, group, slot].astype(jnp.float32)
    d_tokens = jnp.sum(back_rows.reshape(TOKENS, TOPK, D), axis=1).astype(jnp.bfloat16)
    return mixed, d_tokens, d_combine, grad_gate, grad_up, grad_down
```

```python
import functools
import math

import jax
import jax.numpy as jnp
from jax import lax
from jax.experimental import pallas as pl
from jax.experimental.pallas import tpu as pltpu
from jax.sharding import PartitionSpec as P

TOPK = 2
CAP = 20
MESH = pl.DeviceIdType.MESH
EX, HI, MID, LOW = 0, 1, 2, 3
ORDERS = ((HI, MID, EX, LOW), (EX, HI, MID, LOW))


def sizes_of(groups, section):
    return (groups, section // 4, 2, 2)


def place():
    sec = lax.axis_index("section")
    return (
        lax.axis_index("expert"),
        lax.div(sec, 4),
        lax.rem(lax.div(sec, 2), 2),
        lax.rem(sec, 2),
    )


def peer(me, sizes, dim, step):
    there = list(me)
    there[dim] = lax.rem(me[dim] + step, sizes[dim])
    return tuple(there)


def device(where):
    return {"expert": where[EX], "section": (where[HI] * 2 + where[MID]) * 2 + where[LOW]}


def greet(me, sizes):
    barrier = pltpu.get_barrier_semaphore()
    count = 0
    for dim in range(4):
        for step in range(1, sizes[dim]):
            pl.semaphore_signal(
                barrier, inc=1, device_id=device(peer(me, sizes, dim, step)), device_id_type=MESH
            )
            count += 1
    pl.semaphore_wait(barrier, count)


def split_rows(rows):
    if rows % 32 == 0:
        return ((0, rows // 2), (rows // 2, rows // 2))
    return ((0, rows),)


def gather_kernel(sizes, parts, x_ref, info_ref, out_ref, info_out, send, recv, isend, irecv):
    me = place()
    out_ref[me[0], me[1], me[2], me[3]] = x_ref[...]
    info_out[me[EX]] = info_ref[...]
    greet(me, sizes)
    copies = []
    for step in range(1, sizes[EX]):
        copy = pltpu.make_async_remote_copy(
            src_ref=info_ref,
            dst_ref=info_out.at[me[EX]],
            send_sem=isend.at[step - 1],
            recv_sem=irecv.at[step - 1],
            device_id=device(peer(me, sizes, EX, step)),
            device_id_type=MESH,
        )
        copy.start()
        copies.append(copy)
    have = [list(me) for _ in parts]
    before = [[] for _ in parts]
    for stage in range(4):
        for p, (low, rows) in enumerate(parts):
            for copy in before[p]:
                copy.wait_recv()
            dim = ORDERS[p][stage]
            block = out_ref.at[tuple(have[p]) + (pl.ds(low, rows),)]
            before[p] = []
            for step in range(1, sizes[dim]):
                copy = pltpu.make_async_remote_copy(
                    src_ref=block,
                    dst_ref=block,
                    send_sem=send.at[p, stage, step - 1],
                    recv_sem=recv.at[p, stage, step - 1],
                    device_id=device(peer(me, sizes, dim, step)),
                    device_id_type=MESH,
                )
                copy.start()
                before[p].append(copy)
                copies.append(copy)
            have[p][dim] = pl.ds(0, sizes[dim])
    for p in range(len(parts)):
        for copy in before[p]:
            copy.wait_recv()
    for copy in copies[: sizes[EX] - 1]:
        copy.wait_recv()
    for copy in copies:
        copy.wait_send()


def gather(block, info, sizes):
    rows = block.shape[0]
    parts = split_rows(rows)
    most = max(sizes) - 1
    vmem = pl.BlockSpec(memory_space=pltpu.VMEM)
    return pl.pallas_call(
        functools.partial(gather_kernel, sizes, parts),
        out_shape=(
            jax.ShapeDtypeStruct(sizes + block.shape, block.dtype),
            jax.ShapeDtypeStruct((sizes[EX],) + info.shape, info.dtype),
        ),
        in_specs=[vmem, vmem],
        out_specs=(vmem, vmem),
        scratch_shapes=[
            pltpu.SemaphoreType.DMA((len(parts), 4, most)),
            pltpu.SemaphoreType.DMA((len(parts), 4, most)),
            pltpu.SemaphoreType.DMA((most,)),
            pltpu.SemaphoreType.DMA((most,)),
        ],
        compiler_params=pltpu.CompilerParams(
            collective_id=0, has_side_effects=True, vmem_limit_bytes=40 * 2**20
        ),
    )(block, info)


def left_shape(sizes, order, stage):
    gone = order[: stage + 1]
    return tuple(1 if d in gone else sizes[d] for d in range(4))


def scatter_kernel(sizes, parts, p_ref, out_ref, acc, *rest):
    lands = rest[: 4 * len(parts)]
    send, recv = rest[4 * len(parts) :]
    me = place()
    greet(me, sizes)
    keep = [[pl.ds(0, n) for n in sizes] for _ in parts]
    copies = []
    flying = [[] for _ in parts]

    def start(p, stage):
        low, rows = parts[p]
        dim = ORDERS[p][3 - stage]
        source = p_ref if stage == 0 else acc
        flying[p] = []
        for step in range(1, sizes[dim]):
            index = list(keep[p])
            index[dim] = lax.rem(me[dim] + step, sizes[dim])
            index = [pl.ds(i, 1) if not isinstance(i, pl.Slice) else i for i in index]
            copy = pltpu.make_async_remote_copy(
                src_ref=source.at[tuple(index) + (pl.ds(low, rows),)],
                dst_ref=lands[p * 4 + stage].at[step - 1],
                send_sem=send.at[p, stage, step - 1],
                recv_sem=recv.at[p, stage, step - 1],
                device_id=device(peer(me, sizes, dim, step)),
                device_id_type=MESH,
            )
            copy.start()
            flying[p].append(copy)
            copies.append(copy)
        keep[p][dim] = me[dim]

    def add(p, stage):
        low, rows = parts[p]
        for copy in flying[p]:
            copy.wait_recv()
        dim = ORDERS[p][3 - stage]
        source = p_ref if stage == 0 else acc
        land = lands[p * 4 + stage]
        shape = left_shape(sizes, ORDERS[p][::-1], stage)
        gone = ORDERS[p][::-1][: stage + 1]

        def body(j, carry):
            rest_index = []
            left = j
            for d in reversed(range(4)):
                rest_index.append(lax.rem(left, shape[d]))
                left = lax.div(left, shape[d])
            rest_index = rest_index[::-1]
            full = tuple(me[d] if d in gone else rest_index[d] for d in range(4))
            total = source[full + (pl.ds(low, rows),)].astype(jnp.float32)
            for step in range(1, sizes[dim]):
                total += land[(step - 1,) + tuple(rest_index)].astype(jnp.float32)
            total = total.astype(acc.dtype)
            if stage == 3:
                out_ref[pl.ds(low, rows), :] = total
            else:
                acc[full + (pl.ds(low, rows),)] = total
            return carry

        lax.fori_loop(0, math.prod(shape), body, 0)

    for p in range(len(parts)):
        start(p, 0)
    for stage in range(4):
        for p in range(len(parts)):
            add(p, stage)
            if stage < 3:
                start(p, stage + 1)
    for copy in copies:
        copy.wait_send()


def scatter(partial, sizes):
    block = partial.shape[4:]
    parts = split_rows(block[0])
    most = max(sizes) - 1
    lands = []
    for p, (_, rows) in enumerate(parts):
        order = ORDERS[p][::-1]
        for stage in range(4):
            shape = (sizes[order[stage]] - 1,) + left_shape(sizes, order, stage)
            lands.append(pltpu.VMEM(shape + (rows, block[1]), partial.dtype))
    vmem = pl.BlockSpec(memory_space=pltpu.VMEM)
    return pl.pallas_call(
        functools.partial(scatter_kernel, sizes, parts),
        out_shape=jax.ShapeDtypeStruct(block, partial.dtype),
        in_specs=[vmem],
        out_specs=vmem,
        scratch_shapes=[pltpu.VMEM(partial.shape, partial.dtype)]
        + lands
        + [
            pltpu.SemaphoreType.DMA((len(parts), 4, most)),
            pltpu.SemaphoreType.DMA((len(parts), 4, most)),
        ],
        compiler_params=pltpu.CompilerParams(
            collective_id=1, has_side_effects=True, vmem_limit_bytes=40 * 2**20
        ),
    )(partial)


def expert_kernel(
    x_ref, c_ref, s_ref, wg_ref, wu_ref, wd_ref,
    out_ref, din_ref, dc_ref, gg_ref, gu_ref, gd_ref, acc_o, acc_i,
):
    step = pl.program_id(1)
    dot = functools.partial(lax.dot_general, preferred_element_type=jnp.float32)
    nn = (((1,), (0,)), ((), ()))
    nt = (((1,), (1,)), ((), ()))
    tn = (((0,), (0,)), ((), ()))
    x = x_ref[0]
    weight = s_ref[0][:, :1]
    d_out = (c_ref[0].astype(jnp.float32) * weight).astype(jnp.bfloat16)
    gate = dot(x, wg_ref[0], nn)
    up = dot(x, wu_ref[0], nn)
    sig = jax.nn.sigmoid(gate)
    act = gate * sig
    hidden = (act * up).astype(jnp.bfloat16)
    out = dot(hidden, wd_ref[0], nn)
    d_hidden = dot(d_out, wd_ref[0], nt)
    d_gate = (d_hidden * up * sig * (1.0 + gate * (1.0 - sig))).astype(jnp.bfloat16)
    d_up = (d_hidden * act).astype(jnp.bfloat16)
    gd_ref[0] = dot(hidden, d_out, tn).astype(jnp.bfloat16)
    gg_ref[0] = dot(x, d_gate, tn).astype(jnp.bfloat16)
    gu_ref[0] = dot(x, d_up, tn).astype(jnp.bfloat16)
    d_in = dot(d_gate, wg_ref[0], nt) + dot(d_up, wu_ref[0], nt)

    @pl.when(step == 0)
    def _():
        acc_o[...] = out
        acc_i[...] = d_in

    @pl.when(step > 0)
    def _():
        acc_o[...] += out
        acc_i[...] += d_in

    @pl.when(step == pl.num_programs(1) - 1)
    def _():
        whole = acc_o[...]
        out_ref[0] = (whole * weight).astype(jnp.bfloat16)
        din_ref[0] = acc_i[...].astype(jnp.bfloat16)
        dot_rows = jnp.sum(whole * c_ref[0].astype(jnp.float32), axis=1, keepdims=True)
        dc_ref[0] = jnp.broadcast_to(dot_rows, dc_ref.shape[1:])


def experts(x, cot, weight, w_gate, w_up, w_down):
    local, rows, width = x.shape
    hid = w_gate.shape[2]
    part = min(hid, 256)
    row_spec = pl.BlockSpec((1, rows, width), lambda e, h: (e, 0, 0))
    small = pl.BlockSpec((1, rows, 128), lambda e, h: (e, 0, 0))
    wide = pl.BlockSpec((1, width, part), lambda e, h: (e, 0, h))
    tall = pl.BlockSpec((1, part, width), lambda e, h: (e, h, 0))
    return pl.pallas_call(
        expert_kernel,
        grid=(local, hid // part),
        out_shape=(
            jax.ShapeDtypeStruct(x.shape, jnp.bfloat16),
            jax.ShapeDtypeStruct(x.shape, jnp.bfloat16),
            jax.ShapeDtypeStruct((local, rows, 128), jnp.float32),
            jax.ShapeDtypeStruct(w_gate.shape, jnp.bfloat16),
            jax.ShapeDtypeStruct(w_up.shape, jnp.bfloat16),
            jax.ShapeDtypeStruct(w_down.shape, jnp.bfloat16),
        ),
        in_specs=[row_spec, row_spec, small, wide, wide, tall],
        out_specs=(row_spec, row_spec, small, wide, wide, tall),
        scratch_shapes=[
            pltpu.VMEM((rows, width), jnp.float32),
            pltpu.VMEM((rows, width), jnp.float32),
        ],
        compiler_params=pltpu.CompilerParams(vmem_limit_bytes=56 * 2**20),
    )(x, cot, weight, w_gate, w_up, w_down)


def on_device(tokens, routes, combine, w_gate, w_up, w_down, cotangent):
    groups = lax.axis_size("expert")
    section = lax.axis_size("section")
    sizes = sizes_of(groups, section)
    tok, feat = tokens.shape
    width = feat * section
    local = w_gate.shape[0]
    rows = -(-groups * CAP // 16) * 16
    block = jnp.concatenate([tokens, cotangent], axis=0).T
    info = jnp.concatenate([routes.astype(jnp.float32), combine], axis=1).T
    info = jnp.pad(info, ((0, 8 - 2 * TOPK), (0, 128 - tok)))
    gathered, infos = gather(block, info, sizes)
    gathered = gathered.reshape(groups, width, 2 * tok)
    ids = infos[:, :TOPK, :tok].astype(jnp.int32)
    weights = infos[:, TOPK : 2 * TOPK, :tok]
    named = (ids[..., None] == jnp.arange(local * groups, dtype=jnp.int32)).astype(jnp.int32)
    both = jnp.sum(named, axis=1)
    earlier = jnp.cumsum(both, axis=1) - both
    slot = jnp.sum(earlier[:, None] * named, axis=3)
    base = lax.axis_index("expert") * local
    group = jnp.arange(groups, dtype=jnp.int32)[:, None, None]
    code = (ids - base) * rows + group * CAP + slot
    hit = (code[None] == jnp.arange(local * rows, dtype=jnp.int32)[:, None, None, None]).astype(
        jnp.float32
    )
    pick = jnp.sum(hit, axis=2).astype(jnp.bfloat16)
    weight = jnp.sum(hit * weights[None], axis=(1, 2, 3))
    spread = functools.partial(jnp.einsum, "pet,edt->pd", preferred_element_type=jnp.float32)
    x = spread(pick, gathered[:, :, :tok]).astype(jnp.bfloat16).reshape(local, rows, width)
    cot = spread(pick, gathered[:, :, tok:]).astype(jnp.bfloat16).reshape(local, rows, width)
    weight = jnp.broadcast_to(weight.reshape(local, rows, 1), (local, rows, 128))
    out, d_in, d_rows, grad_gate, grad_up, grad_down = experts(
        x, cot, weight, w_gate, w_up, w_down
    )
    collect = functools.partial(jnp.einsum, "pet,pd->edt", preferred_element_type=jnp.float32)
    partial = jnp.concatenate(
        [
            collect(pick, out.reshape(local * rows, width)),
            collect(pick, d_in.reshape(local * rows, width)),
        ],
        axis=2,
    ).astype(jnp.bfloat16)
    d_rows = d_rows[:, :, 0].reshape(-1)
    d_combine = jnp.sum(hit * d_rows[:, None, None, None], axis=0)
    d_combine = lax.psum(d_combine, ("expert", "section"))
    d_combine = lax.dynamic_index_in_dim(
        d_combine, lax.axis_index("expert"), 0, keepdims=False
    ).T
    done = scatter(partial.reshape(sizes + (feat, 2 * tok)), sizes).T
    return (done[:tok], done[tok:], d_combine, grad_gate, grad_up, grad_down)


def solution(mesh):
    placed = (
        P("expert", "section"),
        P("expert", None),
        P("expert", None),
        P("expert", None, "section"),
        P("expert", None, "section"),
        P("expert", "section", None),
        P("expert", "section"),
    )
    return jax.shard_map(
        on_device,
        mesh=mesh,
        in_specs=placed,
        out_specs=(
            P("expert", "section"),
            P("expert", "section"),
            P("expert", None),
            P("expert", None, "section"),
            P("expert", None, "section"),
            P("expert", "section", None),
        ),
        check_vma=False,
    )
```

```python
import functools
import math

import jax
import jax.numpy as jnp
from jax import lax
from jax.experimental import pallas as pl
from jax.experimental.pallas import tpu as pltpu
from jax.sharding import PartitionSpec as P

TOPK = 2
CAP = 20
MESH = pl.DeviceIdType.MESH
EX, HI, MID, LOW = 0, 1, 2, 3
ORDERS = ((HI, MID, EX, LOW), (EX, HI, MID, LOW))


def sizes_of(groups, section):
    return (groups, section // 4, 2, 2)


def place():
    sec = lax.axis_index("section")
    return (
        lax.axis_index("expert"),
        lax.div(sec, 4),
        lax.rem(lax.div(sec, 2), 2),
        lax.rem(sec, 2),
    )


def peer(me, sizes, dim, step):
    there = list(me)
    there[dim] = lax.rem(me[dim] + step, sizes[dim])
    return tuple(there)


def device(where):
    return {"expert": where[EX], "section": (where[HI] * 2 + where[MID]) * 2 + where[LOW]}


def greet(me, sizes):
    barrier = pltpu.get_barrier_semaphore()
    count = 0
    for dim in range(4):
        for step in range(1, sizes[dim]):
            pl.semaphore_signal(
                barrier, inc=1, device_id=device(peer(me, sizes, dim, step)), device_id_type=MESH
            )
            count += 1
    pl.semaphore_wait(barrier, count)


def split_rows(rows):
    if rows % 32 == 0:
        return ((0, rows // 2), (rows // 2, rows // 2))
    return ((0, rows),)


def eye(n):
    row = lax.broadcasted_iota(jnp.int32, (n, n), 0)
    col = lax.broadcasted_iota(jnp.int32, (n, n), 1)
    return jnp.where(row == col, 1.0, 0.0).astype(jnp.bfloat16)


def gather_kernel(sizes, parts, tok_ref, cot_ref, info_ref, out_ref, info_out, send, recv, isend, irecv):
    me = place()
    both = jnp.concatenate([tok_ref[...], cot_ref[...]], axis=0)
    turned = lax.dot_general(
        both, eye(both.shape[0]), (((0,), (0,)), ((), ())), preferred_element_type=jnp.float32
    )
    out_ref[me[0], me[1], me[2], me[3]] = turned.astype(jnp.bfloat16)
    info_out[me[EX]] = info_ref[...]
    greet(me, sizes)
    copies = []
    for step in range(1, sizes[EX]):
        copy = pltpu.make_async_remote_copy(
            src_ref=info_ref,
            dst_ref=info_out.at[me[EX]],
            send_sem=isend.at[step - 1],
            recv_sem=irecv.at[step - 1],
            device_id=device(peer(me, sizes, EX, step)),
            device_id_type=MESH,
        )
        copy.start()
        copies.append(copy)
    have = [list(me) for _ in parts]
    before = [[] for _ in parts]
    for stage in range(4):
        for p, (low, rows) in enumerate(parts):
            for copy in before[p]:
                copy.wait_recv()
            dim = ORDERS[p][stage]
            block = out_ref.at[tuple(have[p]) + (pl.ds(low, rows),)]
            before[p] = []
            for step in range(1, sizes[dim]):
                copy = pltpu.make_async_remote_copy(
                    src_ref=block,
                    dst_ref=block,
                    send_sem=send.at[p, stage, step - 1],
                    recv_sem=recv.at[p, stage, step - 1],
                    device_id=device(peer(me, sizes, dim, step)),
                    device_id_type=MESH,
                )
                copy.start()
                before[p].append(copy)
                copies.append(copy)
            have[p][dim] = pl.ds(0, sizes[dim])
    for p in range(len(parts)):
        for copy in before[p]:
            copy.wait_recv()
    for copy in copies[: sizes[EX] - 1]:
        copy.wait_recv()
    for copy in copies:
        copy.wait_send()


def gather(tokens, cotangent, info, sizes):
    rows = tokens.shape[1]
    parts = split_rows(rows)
    most = max(sizes) - 1
    vmem = pl.BlockSpec(memory_space=pltpu.VMEM)
    return pl.pallas_call(
        functools.partial(gather_kernel, sizes, parts),
        out_shape=(
            jax.ShapeDtypeStruct(sizes + (rows, 2 * tokens.shape[0]), tokens.dtype),
            jax.ShapeDtypeStruct((sizes[EX],) + info.shape, info.dtype),
        ),
        in_specs=[vmem, vmem, vmem],
        out_specs=(vmem, vmem),
        scratch_shapes=[
            pltpu.SemaphoreType.DMA((len(parts), 4, most)),
            pltpu.SemaphoreType.DMA((len(parts), 4, most)),
            pltpu.SemaphoreType.DMA((most,)),
            pltpu.SemaphoreType.DMA((most,)),
        ],
        compiler_params=pltpu.CompilerParams(
            collective_id=0, has_side_effects=True, vmem_limit_bytes=40 * 2**20
        ),
    )(tokens, cotangent, info)


def left_shape(sizes, order, stage):
    gone = order[: stage + 1]
    return tuple(1 if d in gone else sizes[d] for d in range(4))


def scatter_kernel(sizes, parts, p_ref, dc_ref, mixed_ref, dtok_ref, dc_out, acc, out_ref, *rest):
    lands = rest[: 4 * len(parts)]
    small = rest[4 * len(parts) : 4 * len(parts) + 4]
    send, recv, ssend, srecv = rest[4 * len(parts) + 4 :]
    me = place()
    small[0][me[ORDERS[0][3]]] = dc_ref[...]
    greet(me, sizes)
    keep = [[pl.ds(0, n) for n in sizes] for _ in parts]
    copies = []
    flying = [[] for _ in parts]

    def start(p, stage):
        low, rows = parts[p]
        dim = ORDERS[p][3 - stage]
        source = p_ref if stage == 0 else acc
        flying[p] = []
        for step in range(1, sizes[dim]):
            index = list(keep[p])
            index[dim] = lax.rem(me[dim] + step, sizes[dim])
            index = [pl.ds(i, 1) if not isinstance(i, pl.Slice) else i for i in index]
            copy = pltpu.make_async_remote_copy(
                src_ref=source.at[tuple(index) + (pl.ds(low, rows),)],
                dst_ref=lands[p * 4 + stage].at[step - 1],
                send_sem=send.at[p, stage, step - 1],
                recv_sem=recv.at[p, stage, step - 1],
                device_id=device(peer(me, sizes, dim, step)),
                device_id_type=MESH,
            )
            copy.start()
            flying[p].append(copy)
            copies.append(copy)
        keep[p][dim] = me[dim]

    def add(p, stage):
        low, rows = parts[p]
        for copy in flying[p]:
            copy.wait_recv()
        dim = ORDERS[p][3 - stage]
        source = p_ref if stage == 0 else acc
        land = lands[p * 4 + stage]
        shape = left_shape(sizes, ORDERS[p][::-1], stage)
        gone = ORDERS[p][::-1][: stage + 1]

        def body(j, carry):
            rest_index = []
            left = j
            for d in reversed(range(4)):
                rest_index.append(lax.rem(left, shape[d]))
                left = lax.div(left, shape[d])
            rest_index = rest_index[::-1]
            full = tuple(me[d] if d in gone else rest_index[d] for d in range(4))
            total = source[full + (pl.ds(low, rows),)].astype(jnp.float32)
            for step in range(1, sizes[dim]):
                total += land[(step - 1,) + tuple(rest_index)].astype(jnp.float32)
            total = total.astype(acc.dtype)
            if stage == 3:
                out_ref[pl.ds(low, rows), :] = total
            else:
                acc[full + (pl.ds(low, rows),)] = total
            return carry

        lax.fori_loop(0, math.prod(shape), body, 0)

    def start_small(stage):
        dim = ORDERS[0][3 - stage]
        block = small[stage].at[me[dim]]
        started = []
        for step in range(1, sizes[dim]):
            copy = pltpu.make_async_remote_copy(
                src_ref=block,
                dst_ref=block,
                send_sem=ssend.at[stage, step - 1],
                recv_sem=srecv.at[stage, step - 1],
                device_id=device(peer(me, sizes, dim, step)),
                device_id_type=MESH,
            )
            copy.start()
            started.append(copy)
            copies.append(copy)
        return started

    def add_small(stage, started):
        for copy in started:
            copy.wait_recv()
        total = small[stage][0]
        for i in range(1, sizes[ORDERS[0][3 - stage]]):
            total += small[stage][i]
        if stage == 3:
            dc_out[...] = total
        else:
            small[stage + 1][me[ORDERS[0][2 - stage]]] = total

    for p in range(len(parts)):
        start(p, 0)
    started = start_small(0)
    for stage in range(4):
        for p in range(len(parts)):
            add(p, stage)
            if stage < 3:
                start(p, stage + 1)
        add_small(stage, started)
        if stage < 3:
            started = start_small(stage + 1)
    block = out_ref[...]
    turned = lax.dot_general(
        eye(block.shape[1]), block, (((1,), (1,)), ((), ())), preferred_element_type=jnp.float32
    ).astype(jnp.bfloat16)
    tok = mixed_ref.shape[0]
    mixed_ref[...] = turned[:tok]
    dtok_ref[...] = turned[tok:]
    for copy in copies:
        copy.wait_send()


def scatter(partial, d_combine, sizes):
    block = partial.shape[4:]
    parts = split_rows(block[0])
    most = max(sizes) - 1
    lands = []
    for p, (_, rows) in enumerate(parts):
        order = ORDERS[p][::-1]
        for stage in range(4):
            shape = (sizes[order[stage]] - 1,) + left_shape(sizes, order, stage)
            lands.append(pltpu.VMEM(shape + (rows, block[1]), partial.dtype))
    vmem = pl.BlockSpec(memory_space=pltpu.VMEM)
    return pl.pallas_call(
        functools.partial(scatter_kernel, sizes, parts),
        out_shape=(
            jax.ShapeDtypeStruct((block[1] // 2, block[0]), partial.dtype),
            jax.ShapeDtypeStruct((block[1] // 2, block[0]), partial.dtype),
            jax.ShapeDtypeStruct(d_combine.shape, d_combine.dtype),
        ),
        in_specs=[vmem, vmem],
        out_specs=(vmem, vmem, vmem),
        scratch_shapes=[
            pltpu.VMEM(partial.shape, partial.dtype),
            pltpu.VMEM(block, partial.dtype),
        ]
        + lands
        + [
            pltpu.VMEM((sizes[ORDERS[0][3 - stage]],) + d_combine.shape, d_combine.dtype)
            for stage in range(4)
        ]
        + [
            pltpu.SemaphoreType.DMA((len(parts), 4, most)),
            pltpu.SemaphoreType.DMA((len(parts), 4, most)),
            pltpu.SemaphoreType.DMA((4, most)),
            pltpu.SemaphoreType.DMA((4, most)),
        ],
        compiler_params=pltpu.CompilerParams(
            collective_id=1, has_side_effects=True, vmem_limit_bytes=40 * 2**20
        ),
    )(partial, d_combine)


def expert_kernel(
    code_ref, comb_ref, all_ref, wg_ref, wu_ref, wd_ref,
    part_ref, dc_ref, gg_ref, gu_ref, gd_ref,
    x_ref, back_ref, d_ref, w_ref, r_ref, acc_o, acc_i,
):
    expert, step = pl.program_id(0), pl.program_id(1)
    last = pl.num_programs(1) - 1
    dot = functools.partial(lax.dot_general, preferred_element_type=jnp.float32)
    nn = (((1,), (0,)), ((), ()))
    nt = (((1,), (1,)), ((), ()))
    tn = (((0,), (0,)), ((), ()))
    groups = all_ref.shape[0]
    _, local, rows, width = x_ref.shape
    lanes = all_ref.shape[2]
    every = local * rows
    row = lax.broadcasted_iota(jnp.int32, (every, lanes), 0)
    lane = lax.broadcasted_iota(jnp.int32, (every, lanes), 1)

    def hits(g):
        return jnp.where(code_ref[g] == row, 1.0, 0.0)

    def picks(g):
        hit = hits(g)
        pick = hit + pltpu.roll(hit, lanes // 2, 1)
        first = jnp.where(lane < lanes // 2, pick, 0.0)
        return jnp.concatenate([first, pick - first], axis=0).astype(jnp.bfloat16)

    @pl.when((step == 0) & (expert == 0))
    def _():
        weight = jnp.zeros((every, 1), jnp.float32)
        for g in range(groups):
            weight += jnp.sum(hits(g) * comb_ref[g], axis=1, keepdims=True)
        w_ref[...] = jnp.broadcast_to(weight, (every, lanes)).reshape(w_ref.shape)
        found = dot(picks(0), all_ref[0], nt)
        for g in range(1, groups):
            found += dot(picks(g), all_ref[g], nt)
        x_ref[...] = found.astype(jnp.bfloat16).reshape(x_ref.shape)

    @pl.when(step == 0)
    def _():
        d_ref[...] = (
            x_ref[1, expert].astype(jnp.float32) * w_ref[expert][:, :1]
        ).astype(jnp.bfloat16)

    x = x_ref[0, expert]
    d_out = d_ref[...]
    gate = dot(x, wg_ref[0], nn)
    up = dot(x, wu_ref[0], nn)
    sig = jax.nn.sigmoid(gate)
    act = gate * sig
    hidden = (act * up).astype(jnp.bfloat16)
    out = dot(hidden, wd_ref[0], nn)
    d_hidden = dot(d_out, wd_ref[0], nt)
    d_gate = (d_hidden * up * sig * (1.0 + gate * (1.0 - sig))).astype(jnp.bfloat16)
    d_up = (d_hidden * act).astype(jnp.bfloat16)
    gd_ref[0] = dot(hidden, d_out, tn).astype(jnp.bfloat16)
    gg_ref[0] = dot(x, d_gate, tn).astype(jnp.bfloat16)
    gu_ref[0] = dot(x, d_up, tn).astype(jnp.bfloat16)
    d_in = dot(d_gate, wg_ref[0], nt) + dot(d_up, wu_ref[0], nt)

    @pl.when(step == 0)
    def _():
        acc_o[...] = out
        acc_i[...] = d_in

    @pl.when(step > 0)
    def _():
        acc_o[...] += out
        acc_i[...] += d_in

    @pl.when(step == last)
    def _():
        whole = acc_o[...]
        back_ref[0, expert] = (whole * w_ref[expert][:, :1]).astype(jnp.bfloat16)
        back_ref[1, expert] = acc_i[...].astype(jnp.bfloat16)
        dot_rows = jnp.sum(whole * x_ref[1, expert].astype(jnp.float32), axis=1, keepdims=True)
        r_ref[expert] = jnp.broadcast_to(dot_rows, r_ref.shape[1:])

    @pl.when((step == last) & (expert == local - 1))
    def _():
        stack = back_ref[...].reshape(2 * every, width)
        drow = r_ref[...].reshape(every, lanes)
        for g in range(groups):
            part_ref[g] = dot(stack, picks(g), tn).astype(jnp.bfloat16)
            dc_ref[g] = jnp.sum(hits(g) * drow, axis=0, keepdims=True)


def experts(code, comb, gathered, rows, w_gate, w_up, w_down):
    groups, width, lanes = gathered.shape
    local, _, hid = w_gate.shape
    part = min(hid, 256)
    whole = lambda shape: pl.BlockSpec(shape, lambda e, h: (0,) * len(shape))
    wide = pl.BlockSpec((1, width, part), lambda e, h: (e, 0, h))
    tall = pl.BlockSpec((1, part, width), lambda e, h: (e, h, 0))
    return pl.pallas_call(
        expert_kernel,
        grid=(local, hid // part),
        out_shape=(
            jax.ShapeDtypeStruct(gathered.shape, jnp.bfloat16),
            jax.ShapeDtypeStruct((groups, 1, lanes), jnp.float32),
            jax.ShapeDtypeStruct(w_gate.shape, jnp.bfloat16),
            jax.ShapeDtypeStruct(w_up.shape, jnp.bfloat16),
            jax.ShapeDtypeStruct(w_down.shape, jnp.bfloat16),
        ),
        in_specs=[
            whole(code.shape), whole(comb.shape), whole(gathered.shape), wide, wide, tall,
        ],
        out_specs=(
            whole(gathered.shape), whole((groups, 1, lanes)), wide, wide, tall,
        ),
        scratch_shapes=[
            pltpu.VMEM((2, local, rows, width), jnp.bfloat16),
            pltpu.VMEM((2, local, rows, width), jnp.bfloat16),
            pltpu.VMEM((rows, width), jnp.bfloat16),
            pltpu.VMEM((local, rows, lanes), jnp.float32),
            pltpu.VMEM((local, rows, lanes), jnp.float32),
            pltpu.VMEM((rows, width), jnp.float32),
            pltpu.VMEM((rows, width), jnp.float32),
        ],
        compiler_params=pltpu.CompilerParams(vmem_limit_bytes=58 * 2**20),
    )(code, comb, gathered, w_gate, w_up, w_down)


def on_device(tokens, routes, combine, w_gate, w_up, w_down, cotangent):
    groups = lax.axis_size("expert")
    sizes = sizes_of(groups, lax.axis_size("section"))
    tok, feat = tokens.shape
    width = feat * lax.axis_size("section")
    local = w_gate.shape[0]
    rows = -(-groups * CAP // 16) * 16
    info = jnp.concatenate([routes.astype(jnp.float32), combine], axis=1).T
    info = jnp.pad(info, ((0, 8 - 2 * TOPK), (0, 128 - tok)))
    gathered, infos = gather(tokens, cotangent, info, sizes)
    gathered = gathered.reshape(groups, width, 2 * tok)
    ids = infos[:, :TOPK, :tok].astype(jnp.int32)
    weights = infos[:, TOPK : 2 * TOPK, :tok]
    named = (ids[..., None] == jnp.arange(local * groups, dtype=jnp.int32)).astype(jnp.int32)
    both = jnp.sum(named, axis=1)
    earlier = jnp.cumsum(both, axis=1) - both
    slot = jnp.sum(earlier[:, None] * named, axis=3)
    base = lax.axis_index("expert") * local
    group = jnp.arange(groups, dtype=jnp.int32)[:, None, None]
    code = (ids - base) * rows + group * CAP + slot
    code = code.reshape(groups, 1, TOPK * tok)
    comb = weights.reshape(groups, 1, TOPK * tok)
    partial, d_combine, grad_gate, grad_up, grad_down = experts(
        code, comb, gathered, rows, w_gate, w_up, w_down
    )
    short = -(-groups // 8) * 8
    d_combine = jnp.pad(d_combine[:, 0], ((0, short - groups), (0, 0)))
    mixed, d_tokens, d_combine = scatter(
        partial.reshape(sizes + (feat, 2 * tok)), d_combine, sizes
    )
    d_combine = lax.dynamic_index_in_dim(
        d_combine, lax.axis_index("expert"), 0, keepdims=False
    )
    d_combine = d_combine.reshape(TOPK, tok).T
    return (mixed, d_tokens, d_combine, grad_gate, grad_up, grad_down)


def solution(mesh):
    placed = (
        P("expert", "section"),
        P("expert", None),
        P("expert", None),
        P("expert", None, "section"),
        P("expert", None, "section"),
        P("expert", "section", None),
        P("expert", "section"),
    )
    return jax.shard_map(
        on_device,
        mesh=mesh,
        in_specs=placed,
        out_specs=(
            P("expert", "section"),
            P("expert", "section"),
            P("expert", None),
            P("expert", None, "section"),
            P("expert", None, "section"),
            P("expert", "section", None),
        ),
        check_vma=False,
    )
```
